32 devices in a mesh: groups: 2 (over y), panel: 4 (over z), layer: 2 (over x), sub: 2 (over core).
Axes of the slice: x: 2, y: 2, z: 4, core: 2. Of those that a mesh axis runs over, the one named last changes fastest.
Arguments:
- values: float32 [32, 8, 128, 128], P(('groups', 'panel', 'sub'), 'layer'), parts along dimension 0, may hold values from -1 to 1
- columns: int32 [32, 8], P(('groups', 'panel', 'sub'), 'layer'), parts along dimension 0, may hold values from 0 to 15, as said below
Outputs:
- purified: float32 [32, 8, 128, 128], P(('groups', 'panel', 'sub'), 'layer'), parts along dimension 0
The draws below stay inside these ranges and needn't reach their ends.
There are 2 independent parts, one for each index of `groups`. The reference program is written for one: setup_inputs(seed, part) draws one part's arguments, and reference() takes and returns one part's arrays. A program takes and returns all parts, laid end to end along the dimension named above; each array names one. Nothing has to cross between parts.
Inputs may be any that keep to these rules, and one draw needn't show every extreme that they name: Each block row names 8 different block columns; slot 0 of block row i names column i.
All inputs are finite; a program needn't handle non-finite values.
Results may differ from the reference program's by a relative error of at most 0.0003.
Values sent between devices are 32-bit elements; how exact they have to be, the bound alone decides.
A program may use at most 128 MiB of HBM per device.

```python
import jax
import jax.numpy as jnp
from jax import lax

BLK = 128
SLOTS = 8
NB = 16


def draw_columns(key, part):
    key = jax.random.fold_in(key, 11)
    scores = jax.random.randint(key, (NB, NB), 0, 2 ** 20) * NB + jnp.arange(NB, dtype=jnp.int32)[None, :]
    scores = jnp.where(jnp.eye(NB, dtype=bool), 2 ** 30, scores)
    return lax.top_k(scores, SLOTS)[1].astype(jnp.int32)


def draw_values(key, part):
    key = jax.random.fold_in(key, 23)
    spread = 0.4 / (SLOTS * BLK) ** 0.5
    jitter = jax.random.normal(key, (NB, SLOTS, BLK, BLK), jnp.float32)
    centre = 0.5
    identity_matrix = jnp.eye(BLK, dtype=jnp.float32)
    first_slot = (jnp.arange(SLOTS) == 0).astype(jnp.float32)
    return jitter * spread + centre * first_slot[None, :, None, None] * identity_matrix[None, None, :, :]


def setup_inputs(seed: int = 0, part: int = 0) -> dict:
    splits = jax.random.split(jax.random.key(seed), 3)
    part_splits = jax.random.split(jax.random.fold_in(splits[2], part), 3)
    values = draw_values(jax.random.fold_in(jax.random.fold_in(splits[2], part), 71), part)
    columns = draw_columns(jax.random.fold_in(jax.random.fold_in(splits[2], part), 71), part)
    return dict(values=values, columns=columns)


highest_precision = lax.Precision.HIGHEST


def masked_product(left, right, columns):
    def one_row(position):
        own_cols = columns[position]
        left_row = left[position]
        right_rows = right[own_cols]
        right_cols = columns[own_cols]
        block_products = jnp.einsum("uab,usbc->usac", left_row, right_rows, precision=highest_precision)
        target_blocks = (own_cols[:, None, None] == right_cols[None, :, :]).astype(jnp.float32)
        return jnp.einsum("eif,iflq->elq", target_blocks, block_products, precision=highest_precision)
    return lax.map(one_row, jnp.arange(NB, dtype=jnp.int32))


def reference(values, columns):
    square = masked_product(values, values, columns)
    cube = masked_product(square, values, columns)
    return 3.0 * square - 2.0 * cube
```

```python
import jax
import jax.numpy as jnp
from jax import lax
from jax.experimental import pallas as pl
from jax.experimental.pallas import tpu as pltpu
from jax.sharding import PartitionSpec as P

highest_precision = lax.Precision.HIGHEST
MESH = pl.DeviceIdType.MESH


def masked_rows(left_vals, left_cols, right_vals, right_cols):
    block_products = jnp.einsum(
        "ruab,rusbc->rusac", left_vals, right_vals, precision=highest_precision
    )
    target_blocks = (left_cols[:, :, None, None] == right_cols[:, None, :, :]).astype(jnp.float32)
    return jnp.einsum(
        "rtus,rusac->rtac", target_blocks, block_products, precision=highest_precision
    )


def shards_general(values, columns):
    full_vals, full_cols = (
        lax.all_gather(values, "layer", axis=1, tiled=True),
        lax.all_gather(columns, "layer", axis=1, tiled=True),
    )
    slab_pieces = (
        lax.all_gather(values, ("panel", "sub"), axis=0, tiled=True),
        lax.all_gather(columns, ("panel", "sub"), axis=0, tiled=True),
    )
    kept_vals = slab_pieces[0][full_cols]
    kept_cols = slab_pieces[1][full_cols]
    square_part = masked_rows(full_vals, full_cols, kept_vals, kept_cols)
    square_own = lax.psum_scatter(square_part, "layer", scatter_dimension=1, tiled=True)
    square_full = lax.all_gather(square_own, "layer", axis=1, tiled=True)
    cube_part = masked_rows(square_full, full_cols, kept_vals, kept_cols)
    cube_own = lax.psum_scatter(cube_part, "layer", scatter_dimension=1, tiled=True)
    return 3.0 * square_own - 2.0 * cube_own


def kernel(tile_ref, v_ref, o_ref, xbuf, hi, lo, sq, tq, tz, tabs,
           send_sem, recv_own, recv_sib, tsend, trecv, local_sem):
    z = lax.axis_index("panel")
    x = lax.axis_index("layer")
    c = lax.axis_index("sub")
    xo, co = 1 - x, 1 - c
    rows, half, blk, _ = v_ref.shape
    slots = 2 * half
    zero_block = hi.shape[0] - 1

    far = z // 2
    zm = z + far * (3 - 2 * z)
    is_end = zm == 0
    is_mid = zm == 1

    def plane(q):
        return q + far * (3 - 2 * q)

    q_list = [plane(zm), plane(1 - zm), plane(2), plane(3)]
    z_out = plane(jnp.maximum(zm - 1, 0))
    z_in = plane(zm + 1)

    barrier = pltpu.get_barrier_semaphore()
    others = [lax.rem(z + d, 4) for d in (1, 2, 3)]
    for dev in ({"sub": co}, {"layer": xo}, *({"panel": zz} for zz in others)):
        pl.semaphore_signal(barrier, inc=1, device_id=dev, device_id_type=MESH)
    pl.semaphore_wait(barrier, 5)

    def piece(zz, xx, cc, r):
        return xbuf.at[(zz * 2 + cc) * rows + r, pl.ds(xx * half, half)]

    def number(zz, xx, r):
        return (zz * 2 + xx) * rows + r

    sends = []

    def send(pred, src, zz, xx, r, dev, sib=False):
        slot = len(sends)
        recv = recv_sib if sib else recv_own
        copy = pltpu.make_async_remote_copy(
            src_ref=src,
            dst_ref=piece(zz, xx, c, r),
            send_sem=send_sem.at[slot],
            recv_sem=recv.at[number(zz, xx, r)],
            device_id=dev,
            device_id_type=MESH,
        )
        sends.append((pred, copy))
        if pred is None:
            copy.start()
        else:
            pl.when(pred)(copy.start)

    def wait_piece(zz, xx, cc, r, sem):
        dst = piece(zz, xx, cc, r)
        pltpu.make_async_remote_copy(
            src_ref=dst, dst_ref=dst, send_sem=send_sem.at[0],
            recv_sem=sem.at[number(zz, xx, r)],
            device_id={"sub": co}, device_id_type=MESH,
        ).wait_recv()

    def small(src, dst, s, r, dev):
        return pltpu.make_async_remote_copy(
            src_ref=src, dst_ref=dst, send_sem=tsend.at[s], recv_sem=trecv.at[r],
            device_id=dev, device_id_type=MESH,
        )

    tq[x, c] = tile_ref[...]
    t1 = small(tq.at[x, c], tq.at[x, c], 0, 0, {"sub": co})
    t1.start()

    for r in range(rows):
        own = v_ref.at[r]
        send(None, own, z, x, r, {"panel": z_in})
        send(is_mid, own, z, x, r, {"panel": z_out})
        send(None, own, z, x, r, {"layer": xo})
        send(None, own, z, x, r, {"sub": co}, sib=True)

    t1.wait_recv()
    t2 = small(tq.at[x], tq.at[x], 1, 1, {"layer": xo})
    t2.start()

    for r in range(rows):
        xbuf[(z * 2 + c) * rows + r, pl.ds(x * half, half)] = v_ref[r]
    hi[zero_block] = jnp.zeros((blk, blk), jnp.bfloat16)
    lo[zero_block] = jnp.zeros((blk, blk), jnp.bfloat16)
    sq[...] = jnp.zeros_like(sq)

    t2.wait_recv()
    tz[z] = tq[0] + tq[1]
    t3 = [
        small(tz.at[z], tz.at[z], 2 + d, 2 + z, {"panel": others[d]}) for d in range(3)
    ]
    for t in t3:
        t.start()

    def arrive(q, other, r):
        zz = q_list[q]
        if not other:
            wait_piece(zz, x, c, r, recv_own)
            src = piece(zz, x, c, r)
            if q == 1:
                send(is_mid, src, zz, x, r, {"panel": z_in})
                if r == 0:
                    send(is_end, src, zz, x, r, {"layer": xo})
            else:
                send(is_mid, src, zz, x, r, {"panel": z_out})
                send(None, src, zz, x, r, {"layer": xo})
            send(None, src, zz, x, r, {"sub": co}, sib=True)
        else:
            wait_piece(zz, xo, c, r, recv_own)
            src = piece(zz, xo, c, r)
            if q == 0:
                send(is_end, src, zz, xo, r, {"panel": z_in})
            send(None, src, zz, xo, r, {"sub": co}, sib=True)

    def late_extra():
        r = rows - 1
        send(is_mid, piece(z, xo, c, r), z, xo, r, {"panel": z_out})

    def convert(row):
        val = xbuf[row]
        top = val.astype(jnp.bfloat16)
        hi[pl.ds(row * slots, slots)] = top
        lo[pl.ds(row * slots, slots)] = (val - top.astype(jnp.float32)).astype(jnp.bfloat16)

    def block_at(zz, cc, r, col):
        found = tabs[zz, cc, r, col]
        row = (zz * 2 + cc) * rows + r
        return jnp.where(found > 0, row * slots + found - 1, zero_block)

    def chunk_ready(q, r):
        zz = q_list[q]
        for xx in (x, xo):
            wait_piece(zz, xx, co, r, recv_sib)
        for cc in range(2):
            convert((zz * 2 + cc) * rows + r)

    def times(lh, ll, wh, wl):
        m = lh.shape[0]
        both = jnp.dot(jnp.concatenate([lh, ll], axis=0), wh, preferred_element_type=jnp.float32)
        return both[:m] + both[m:] + jnp.dot(lh, wl, preferred_element_type=jnp.float32)

    def chunk(q, r):
        zz = q_list[q]

        def one_row(i, carry):
            lidx = [block_at(z, c, i, (zz * 2 + cc) * rows + r) for cc in range(2)]
            lh = jnp.concatenate([hi[n] for n in lidx], axis=1)
            ll = jnp.concatenate([lo[n] for n in lidx], axis=1)
            for tp in range(slots // 2):
                ridx = [
                    [block_at(zz, cc, r, tabs[z, c, 2 + i, 2 * tp + e]) for cc in range(2)]
                    for e in range(2)
                ]
                wh = jnp.concatenate(
                    [jnp.concatenate([hi[n] for n in col], axis=0) for col in ridx], axis=1)
                wl = jnp.concatenate(
                    [jnp.concatenate([lo[n] for n in col], axis=0) for col in ridx], axis=1)
                sq[i, tp] += times(lh, ll, wh, wl)
            return carry

        lax.fori_loop(0, rows, one_row, 0)

    arrive(1, False, 0)
    arrive(0, True, 0)
    arrive(1, False, 1)
    arrive(0, True, 1)
    for zz, s in zip(others, range(3)):
        small(tz.at[zz], tz.at[zz], 2, 2 + zz, {"sub": co}).wait_recv()
    stage = pltpu.make_async_copy(tz, tabs, local_sem)
    stage.start()
    chunk_ready(0, 0)
    chunk_ready(0, 1)
    stage.wait()
    chunk(0, 0)
    arrive(2, False, 0)
    arrive(2, False, 1)
    chunk(0, 1)
    arrive(1, True, 0)
    chunk_ready(1, 0)
    chunk(1, 0)
    arrive(2, True, 0)
    chunk_ready(2, 0)
    arrive(3, False, 0)
    chunk(2, 0)
    arrive(2, True, 1)
    chunk_ready(2, 1)
    arrive(3, False, 1)
    late_extra()
    chunk(2, 1)
    arrive(3, True, 0)
    chunk_ready(3, 0)
    chunk(3, 0)
    arrive(3, True, 1)
    arrive(1, True, 1)
    chunk_ready(3, 1)
    chunk(3, 1)
    chunk_ready(1, 1)
    chunk(1, 1)

    def cube_row(i, carry):
        full = jnp.concatenate([sq[i, tp] for tp in range(slots // 2)], axis=1)
        sh = full.astype(jnp.bfloat16)
        sl = (full - sh.astype(jnp.float32)).astype(jnp.bfloat16)
        ks = [tabs[z, c, 2 + i, u] for u in range(slots)]
        for e in range(half // 2):
            cols = [tabs[z, c, 2 + i, x * half + 2 * e + f] for f in range(2)]
            idx = []
            for col in cols:
                one = []
                for k in ks:
                    found = tabs[k // (2 * rows), (k // rows) % 2, k % rows, col]
                    one.append(jnp.where(found > 0, k * slots + found - 1, zero_block))
                idx.append(one)
            wh = jnp.concatenate(
                [jnp.concatenate([hi[n] for n in one], axis=0) for one in idx], axis=1)
            wl = jnp.concatenate(
                [jnp.concatenate([lo[n] for n in one], axis=0) for one in idx], axis=1)
            res = 3.0 * sq[i, x * (half // 2) + e] - 2.0 * times(sh, sl, wh, wl)
            o_ref[i, 2 * e] = res[:, :blk]
            o_ref[i, 2 * e + 1] = res[:, blk:]
        return carry

    lax.fori_loop(0, rows, cube_row, 0)

    for t in (t1, t2, *t3):
        t.wait_send()
    for pred, copy in sends:
        if pred is None:
            copy.wait_send()
        else:
            pl.when(pred)(copy.wait_send)


def shards_kernel(values, columns):
    rows, half, blk, _ = values.shape
    slots, nb = 2 * half, 8 * rows
    x = lax.axis_index("layer")
    lanes = jnp.arange(128, dtype=jnp.int32)
    place = jnp.arange(half, dtype=jnp.int32) + x * half
    by_col = jnp.sum(
        jnp.where(columns[:, :, None] == lanes, place[None, :, None] + 1, 0), axis=1)
    by_slot = jnp.sum(
        jnp.where(place[None, :, None] == lanes, columns[:, :, None], 0), axis=1)
    tile = jnp.concatenate(
        [by_col, by_slot, jnp.zeros((8 - 2 * rows, 128), jnp.int32)], axis=0).astype(jnp.int32)
    vmem = pl.BlockSpec(memory_space=pltpu.VMEM)
    return pl.pallas_call(
        kernel,
        out_shape=jax.ShapeDtypeStruct(values.shape, jnp.float32),
        in_specs=[vmem, vmem],
        out_specs=vmem,
        scratch_shapes=[
            pltpu.VMEM((nb, slots, blk, blk), jnp.float32),
            pltpu.VMEM((nb * slots + 1, blk, blk), jnp.bfloat16),
            pltpu.VMEM((nb * slots + 1, blk, blk), jnp.bfloat16),
            pltpu.VMEM((rows, slots // 2, blk, 2 * blk), jnp.float32),
            pltpu.VMEM((2, 2, 8, 128), jnp.int32),
            pltpu.VMEM((4, 2, 8, 128), jnp.int32),
            pltpu.SMEM((4, 2, 8, 128), jnp.int32),
            pltpu.SemaphoreType.DMA((36,)),
            pltpu.SemaphoreType.DMA((4 * 2 * rows,)),
            pltpu.SemaphoreType.DMA((4 * 2 * rows,)),
            pltpu.SemaphoreType.DMA((5,)),
            pltpu.SemaphoreType.DMA((6,)),
            pltpu.SemaphoreType.DMA,
        ],
        compiler_params=pltpu.CompilerParams(
            collective_id=0, has_side_effects=True, vmem_limit_bytes=48 * 1024 * 1024,
        ),
        cost_estimate=pl.CostEstimate(
            flops=3 * 2 * 3 * 64 * 2 * blk ** 3, bytes_accessed=2 * values.size * 4,
            transcendentals=0),
    )(tile, values)


def solution(mesh):
    shape = dict(mesh.shape)

    def shards(values, columns):
        fits = (shape["panel"], shape["layer"], shape["sub"]) == (4, 2, 2)
        if fits and values.shape == (2, 4, 128, 128):
            return shards_kernel(values, columns)
        return shards_general(values, columns)

    return jax.shard_map(
        shards,
        mesh=mesh,
        in_specs=(
            P(("groups", "panel", "sub"), "layer", None, None),
            P(("groups", "panel", "sub"), "layer"),
        ),
        out_specs=P(("groups", "panel", "sub"), "layer", None, None),
        check_vma=False,
    )
```

```python
import jax
import jax.numpy as jnp
from jax import lax
from jax.experimental import pallas as pl
from jax.experimental.pallas import tpu as pltpu
from jax.sharding import PartitionSpec as P

highest_precision = lax.Precision.HIGHEST
MESH = pl.DeviceIdType.MESH


def masked_rows(left_vals, left_cols, right_vals, right_cols):
    block_products = jnp.einsum(
        "ruab,rusbc->rusac", left_vals, right_vals, precision=highest_precision
    )
    target_blocks = (left_cols[:, :, None, None] == right_cols[:, None, :, :]).astype(jnp.float32)
    return jnp.einsum(
        "rtus,rusac->rtac", target_blocks, block_products, precision=highest_precision
    )


def shards_general(values, columns):
    full_vals, full_cols = (
        lax.all_gather(values, "layer", axis=1, tiled=True),
        lax.all_gather(columns, "layer", axis=1, tiled=True),
    )
    slab_pieces = (
        lax.all_gather(values, ("panel", "sub"), axis=0, tiled=True),
        lax.all_gather(columns, ("panel", "sub"), axis=0, tiled=True),
    )
    kept_vals = slab_pieces[0][full_cols]
    kept_cols = slab_pieces[1][full_cols]
    square_part = masked_rows(full_vals, full_cols, kept_vals, kept_cols)
    square_own = lax.psum_scatter(square_part, "layer", scatter_dimension=1, tiled=True)
    square_full = lax.all_gather(square_own, "layer", axis=1, tiled=True)
    cube_part = masked_rows(square_full, full_cols, kept_vals, kept_cols)
    cube_own = lax.psum_scatter(cube_part, "layer", scatter_dimension=1, tiled=True)
    return 3.0 * square_own - 2.0 * cube_own


def kernel(tile_ref, v_ref, o_ref, xbuf, hi, lo, sq, ob, tq, tz, tabs,
           send_sem, recv_own, recv_sib, tsend, trecv, local_sem, own_sem, out_sem):
    z = lax.axis_index("panel")
    x = lax.axis_index("layer")
    c = lax.axis_index("sub")
    xo, co = 1 - x, 1 - c
    rows, half, blk, _ = v_ref.shape
    slots = 2 * half
    part = half // 2
    zero_block = hi.shape[0] - 1

    far = z // 2
    zm = z + far * (3 - 2 * z)
    is_end = zm == 0
    is_mid = zm == 1

    def plane(q):
        return q + far * (3 - 2 * q)

    q_list = [plane(zm), plane(1 - zm), plane(2), plane(3)]
    z_out = plane(jnp.maximum(zm - 1, 0))
    z_in = plane(zm + 1)

    barrier = pltpu.get_barrier_semaphore()
    others = [lax.rem(z + d, 4) for d in (1, 2, 3)]
    for dev in ({"sub": co}, {"layer": xo}, *({"panel": zz} for zz in others)):
        pl.semaphore_signal(barrier, inc=1, device_id=dev, device_id_type=MESH)
    pl.semaphore_wait(barrier, 5)

    def piece(zz, xx, cc, r, h):
        return xbuf.at[(zz * 2 + cc) * rows + r, pl.ds(xx * half + h * part, part)]

    def number(zz, xx, r, h):
        return ((zz * 2 + xx) * rows + r) * 2 + h

    sends = []

    def both(p, q):
        return q if p is None else p if q is None else p & q

    def send(pred, src, zz, xx, r, h, dev, sib=False):
        slot = len(sends)
        recv = recv_sib if sib else recv_own
        copy = pltpu.make_async_remote_copy(
            src_ref=src,
            dst_ref=piece(zz, xx, c, r, h),
            send_sem=send_sem.at[slot],
            recv_sem=recv.at[number(zz, xx, r, h)],
            device_id=dev,
            device_id_type=MESH,
        )
        sends.append((pred, copy))
        if pred is None:
            copy.start()
        else:
            pl.when(pred)(copy.start)

    def wait_piece(zz, xx, cc, r, h, sem, pred=None):
        dst = piece(zz, xx, cc, r, h)
        copy = pltpu.make_async_remote_copy(
            src_ref=dst, dst_ref=dst, send_sem=send_sem.at[0],
            recv_sem=sem.at[number(zz, xx, r, h)],
            device_id={"sub": co}, device_id_type=MESH,
        )
        if pred is None:
            copy.wait_recv()
        else:
            pl.when(pred)(copy.wait_recv)

    def small(src, dst, s, r, dev):
        return pltpu.make_async_remote_copy(
            src_ref=src, dst_ref=dst, send_sem=tsend.at[s], recv_sem=trecv.at[r],
            device_id=dev, device_id_type=MESH,
        )

    own = []
    for r in range(rows):
        for h in range(2):
            src = v_ref.at[r, pl.ds(h * part, part)]
            send(None, src, z, x, r, h, {"panel": z_in})
            send(is_mid, src, z, x, r, h, {"panel": z_out})
            send(None, src, z, x, r, h, {"layer": xo})
            send(None, src, z, x, r, h, {"sub": co}, sib=True)
            if r == 0 and h == 0:
                tq[x, c] = tile_ref[...]
                t1 = small(tq.at[x, c], tq.at[x, c], 0, 0, {"sub": co})
                t1.start()
    for r in range(rows):
        own.append(pltpu.make_async_copy(
            v_ref.at[r], xbuf.at[(z * 2 + c) * rows + r, pl.ds(x * half, half)], own_sem.at[r]))
        own[r].start()

    t1.wait_recv()
    t2 = small(tq.at[x], tq.at[x], 1, 1, {"layer": xo})
    t2.start()

    hi[zero_block] = jnp.zeros((blk, blk), jnp.bfloat16)
    lo[zero_block] = jnp.zeros((blk, blk), jnp.bfloat16)
    sq[...] = jnp.zeros_like(sq)

    t2.wait_recv()
    tz[z] = tq[0] + tq[1]
    t3 = [
        small(tz.at[z], tz.at[z], 2 + d, 2 + z, {"panel": others[d]}) for d in range(3)
    ]
    for t in t3:
        t.start()

    def arrive(q, other, r, h, pred=None):
        zz = q_list[q]
        xx = xo if other else x
        wait_piece(zz, xx, c, r, h, recv_own, pred)
        src = piece(zz, xx, c, r, h)

        def pass_on(p, dev, sib=False):
            if p is None or pred is None or p is not pred:
                p = both(p, pred)
            send(p, src, zz, xx, r, h, dev, sib)

        if other:
            if q == 0:
                pass_on(is_end, {"panel": z_in})
        elif q == 1:
            pass_on(is_mid, {"panel": z_in})
            if r == 0:
                pass_on(is_end, {"layer": xo})
        else:
            if pred is not is_end:
                pass_on(is_mid, {"panel": z_out})
            pass_on(None, {"layer": xo})
        pass_on(None, {"sub": co}, sib=True)

    def group(*pieces, pred=None):
        for h in range(2):
            for q, other, r in pieces:
                arrive(q, other, r, h, pred)

    def late_extra():
        r = rows - 1
        for h in range(2):
            send(is_mid, piece(z, xo, c, r, h), z, xo, r, h, {"panel": z_out})

    def convert(row):
        val = xbuf[row]
        top = val.astype(jnp.bfloat16)
        hi[pl.ds(row * slots, slots)] = top
        lo[pl.ds(row * slots, slots)] = (val - top.astype(jnp.float32)).astype(jnp.bfloat16)

    def block_at(zz, cc, r, col):
        found = tabs[zz, cc, r, col]
        row = (zz * 2 + cc) * rows + r
        return jnp.where(found > 0, row * slots + found - 1, zero_block)

    def chunk_ready(q, r):
        zz = q_list[q]
        for xx in (x, xo):
            for h in range(2):
                wait_piece(zz, xx, co, r, h, recv_sib)
        for cc in range(2):
            convert((zz * 2 + cc) * rows + r)

    def times(lh, ll, wh, wl):
        m = lh.shape[0]
        top = jnp.dot(jnp.concatenate([lh, ll], axis=0), wh, preferred_element_type=jnp.float32)
        return top[:m] + top[m:] + jnp.dot(lh, wl, preferred_element_type=jnp.float32)

    def chunk(*parts):
        from_rows = [(q_list[q], cc, r) for q, r in parts for cc in range(2)]

        def one_row(i, carry):
            lidx = [block_at(z, c, i, (zz * 2 + cc) * rows + r) for zz, cc, r in from_rows]
            lh = jnp.concatenate([hi[n] for n in lidx], axis=1)
            ll = jnp.concatenate([lo[n] for n in lidx], axis=1)
            for tp in range(slots // 2):
                cols = [tabs[z, c, 2 + i, 2 * tp + e] for e in range(2)]
                ridx = [[block_at(*row, col) for row in from_rows] for col in cols]
                wh = jnp.concatenate(
                    [jnp.concatenate([hi[n] for n in one], axis=0) for one in ridx], axis=1)
                wl = jnp.concatenate(
                    [jnp.concatenate([lo[n] for n in one], axis=0) for one in ridx], axis=1)
                sq[i, tp] += times(lh, ll, wh, wl)
            return carry

        lax.fori_loop(0, rows, one_row, 0)

    group((1, False, 0), (0, True, 0))
    group((2, False, 0), pred=is_mid)
    group((1, False, 1), (0, True, 1))
    group((2, False, 1), pred=is_mid)
    for zz in others:
        small(tz.at[zz], tz.at[zz], 2, 2 + zz, {"sub": co}).wait_recv()
    stage = pltpu.make_async_copy(tz, tabs, local_sem)
    stage.start()
    for r in range(rows):
        own[r].wait()
    chunk_ready(0, 0)
    chunk_ready(0, 1)
    stage.wait()
    group((2, False, 0), pred=is_end)
    chunk((0, 0), (0, 1))
    group((1, True, 0))
    group((3, False, 0), pred=is_mid)
    group((2, False, 1), pred=is_end)
    chunk_ready(1, 0)
    chunk((1, 0))
    group((2, True, 0))
    group((3, False, 1), pred=is_mid)
    late_extra()
    group((3, False, 0), pred=is_end)
    chunk_ready(2, 0)
    chunk((2, 0))
    group((2, True, 1))
    group((3, False, 1), pred=is_end)
    group((1, True, 1), pred=is_mid)
    chunk_ready(2, 1)
    chunk((2, 1))
    group((3, True, 0))
    chunk_ready(3, 0)
    chunk((3, 0))
    group((1, True, 1), pred=is_end)
    group((3, True, 1))
    chunk_ready(1, 1)
    chunk_ready(3, 1)
    chunk((3, 1), (1, 1))

    def cube_row(i):
        full = jnp.concatenate([sq[i, tp] for tp in range(slots // 2)], axis=1)
        sh = full.astype(jnp.bfloat16)
        sl = (full - sh.astype(jnp.float32)).astype(jnp.bfloat16)
        ks = [tabs[z, c, 2 + i, u] for u in range(slots)]
        for e in range(half // 2):
            cols = [tabs[z, c, 2 + i, x * half + 2 * e + f] for f in range(2)]
            idx = []
            for col in cols:
                one = []
                for k in ks:
                    found = tabs[k // (2 * rows), (k // rows) % 2, k % rows, col]
                    one.append(jnp.where(found > 0, k * slots + found - 1, zero_block))
                idx.append(one)
            wh = jnp.concatenate(
                [jnp.concatenate([hi[n] for n in one], axis=0) for one in idx], axis=1)
            wl = jnp.concatenate(
                [jnp.concatenate([lo[n] for n in one], axis=0) for one in idx], axis=1)
            res = 3.0 * sq[i, x * (half // 2) + e] - 2.0 * times(sh, sl, wh, wl)
            ob[i, 2 * e] = res[:, :blk]
            ob[i, 2 * e + 1] = res[:, blk:]

    outs = []
    for i in range(rows):
        cube_row(i)
        outs.append(pltpu.make_async_copy(ob.at[i], o_ref.at[i], out_sem.at[i]))
        outs[i].start()

    for t in (t1, t2, *t3):
        t.wait_send()
    for pred, copy in sends:
        if pred is None:
            copy.wait_send()
        else:
            pl.when(pred)(copy.wait_send)
    for i in range(rows):
        outs[i].wait()


def shards_kernel(values, columns):
    rows, half, blk, _ = values.shape
    slots, nb = 2 * half, 8 * rows
    x = lax.axis_index("layer")
    lanes = jnp.arange(128, dtype=jnp.int32)
    place = jnp.arange(half, dtype=jnp.int32) + x * half
    by_col = jnp.sum(
        jnp.where(columns[:, :, None] == lanes, place[None, :, None] + 1, 0), axis=1)
    by_slot = jnp.sum(
        jnp.where(place[None, :, None] == lanes, columns[:, :, None], 0), axis=1)
    tile = jnp.concatenate(
        [by_col, by_slot, jnp.zeros((8 - 2 * rows, 128), jnp.int32)], axis=0).astype(jnp.int32)
    vmem = pl.BlockSpec(memory_space=pltpu.VMEM)
    return pl.pallas_call(
        kernel,
        out_shape=jax.ShapeDtypeStruct(values.shape, jnp.float32),
        in_specs=[vmem, pl.BlockSpec(memory_space=pl.ANY)],
        out_specs=pl.BlockSpec(memory_space=pl.ANY),
        scratch_shapes=[
            pltpu.VMEM((nb, slots, blk, blk), jnp.float32),
            pltpu.VMEM((nb * slots + 1, blk, blk), jnp.bfloat16),
            pltpu.VMEM((nb * slots + 1, blk, blk), jnp.bfloat16),
            pltpu.VMEM((rows, slots // 2, blk, 2 * blk), jnp.float32),
            pltpu.VMEM(values.shape, jnp.float32),
            pltpu.VMEM((2, 2, 8, 128), jnp.int32),
            pltpu.VMEM((4, 2, 8, 128), jnp.int32),
            pltpu.SMEM((4, 2, 8, 128), jnp.int32),
            pltpu.SemaphoreType.DMA((96,)),
            pltpu.SemaphoreType.DMA((4 * 2 * rows * 2,)),
            pltpu.SemaphoreType.DMA((4 * 2 * rows * 2,)),
            pltpu.SemaphoreType.DMA((5,)),
            pltpu.SemaphoreType.DMA((6,)),
            pltpu.SemaphoreType.DMA,
            pltpu.SemaphoreType.DMA((rows,)),
            pltpu.SemaphoreType.DMA((rows,)),
        ],
        compiler_params=pltpu.CompilerParams(
            collective_id=0, has_side_effects=True, vmem_limit_bytes=48 * 1024 * 1024,
        ),
        cost_estimate=pl.CostEstimate(
            flops=3 * 2 * 3 * 64 * 2 * blk ** 3, bytes_accessed=2 * values.size * 4,
            transcendentals=0),
    )(tile, values)


def solution(mesh):
    shape = dict(mesh.shape)

    def shards(values, columns):
        fits = (shape["panel"], shape["layer"], shape["sub"]) == (4, 2, 2)
        if fits and values.shape == (2, 4, 128, 128):
            return shards_kernel(values, columns)
        return shards_general(values, columns)

    return jax.shard_map(
        shards,
        mesh=mesh,
        in_specs=(
            P(("groups", "panel", "sub"), "layer", None, None),
            P(("groups", "panel", "sub"), "layer"),
        ),
        out_specs=P(("groups", "panel", "sub"), "layer", None, None),
        check_vma=False,
    )
```

```python
import jax
import jax.numpy as jnp
from jax import lax
from jax.experimental import pallas as pl
from jax.experimental.pallas import tpu as pltpu
from jax.sharding import PartitionSpec as P

highest_precision = lax.Precision.HIGHEST
MESH = pl.DeviceIdType.MESH


def masked_rows(left_vals, left_cols, right_vals, right_cols):
    block_products = jnp.einsum(
        "ruab,rusbc->rusac", left_vals, right_vals, precision=highest_precision
    )
    target_blocks = (left_cols[:, :, None, None] == right_cols[:, None, :, :]).astype(jnp.float32)
    return jnp.einsum(
        "rtus,rusac->rtac", target_blocks, block_products, precision=highest_precision
    )


def shards_general(values, columns):
    full_vals, full_cols = (
        lax.all_gather(values, "layer", axis=1, tiled=True),
        lax.all_gather(columns, "layer", axis=1, tiled=True),
    )
    slab_pieces = (
        lax.all_gather(values, ("panel", "sub"), axis=0, tiled=True),
        lax.all_gather(columns, ("panel", "sub"), axis=0, tiled=True),
    )
    kept_vals = slab_pieces[0][full_cols]
    kept_cols = slab_pieces[1][full_cols]
    square_part = masked_rows(full_vals, full_cols, kept_vals, kept_cols)
    square_own = lax.psum_scatter(square_part, "layer", scatter_dimension=1, tiled=True)
    square_full = lax.all_gather(square_own, "layer", axis=1, tiled=True)
    cube_part = masked_rows(square_full, full_cols, kept_vals, kept_cols)
    cube_own = lax.psum_scatter(cube_part, "layer", scatter_dimension=1, tiled=True)
    return 3.0 * square_own - 2.0 * cube_own


def kernel(cols_ref, v_ref, o_ref, xbuf, hi, lo, sq, tq, tz, tabs,
           send_sem, recv_own, recv_sib, tsend, trecv, local_sem, own_sem):
    z = lax.axis_index("panel")
    x = lax.axis_index("layer")
    c = lax.axis_index("sub")
    xo, co = 1 - x, 1 - c
    rows, half, blk, _ = v_ref.shape
    slots = 2 * half
    part = half // 2
    zero_block = hi.shape[0] - 1

    far = z // 2
    zm = z + far * (3 - 2 * z)
    is_end = zm == 0
    is_mid = zm == 1

    def plane(q):
        return q + far * (3 - 2 * q)

    q_list = [plane(zm), plane(1 - zm), plane(2), plane(3)]
    z_out = plane(jnp.maximum(zm - 1, 0))
    z_in = plane(zm + 1)

    barrier = pltpu.get_barrier_semaphore()
    others = [lax.rem(z + d, 4) for d in (1, 2, 3)]
    for dev in ({"sub": co}, {"layer": xo}, *({"panel": zz} for zz in others)):
        pl.semaphore_signal(barrier, inc=1, device_id=dev, device_id_type=MESH)
    pl.semaphore_wait(barrier, 5)

    def piece(zz, xx, cc, r, h):
        return xbuf.at[(zz * 2 + cc) * rows + r, pl.ds(xx * half + h * part, part)]

    def number(zz, xx, r, h):
        return ((zz * 2 + xx) * rows + r) * 2 + h

    sends = []

    def row_piece(zz, xx, cc, r):
        return xbuf.at[(zz * 2 + cc) * rows + r, pl.ds(xx * half, half)]

    def send_sib(pred, src, zz, xx, r):
        copy = pltpu.make_async_remote_copy(
            src_ref=src,
            dst_ref=row_piece(zz, xx, c, r),
            send_sem=send_sem.at[len(sends)],
            recv_sem=recv_sib.at[(zz * 2 + xx) * rows + r],
            device_id={"sub": co},
            device_id_type=MESH,
        )
        sends.append((pred, copy))
        if pred is None:
            copy.start()
        else:
            pl.when(pred)(copy.start)

    def both(p, q):
        return q if p is None else p if q is None else p & q

    def send(pred, src, zz, xx, r, h, dev):
        slot = len(sends)
        copy = pltpu.make_async_remote_copy(
            src_ref=src,
            dst_ref=piece(zz, xx, c, r, h),
            send_sem=send_sem.at[slot],
            recv_sem=recv_own.at[number(zz, xx, r, h)],
            device_id=dev,
            device_id_type=MESH,
        )
        sends.append((pred, copy))
        if pred is None:
            copy.start()
        else:
            pl.when(pred)(copy.start)

    def wait_piece(zz, xx, r, h, pred=None):
        dst = piece(zz, xx, c, r, h)
        copy = pltpu.make_async_remote_copy(
            src_ref=dst, dst_ref=dst, send_sem=send_sem.at[0],
            recv_sem=recv_own.at[number(zz, xx, r, h)],
            device_id={"sub": co}, device_id_type=MESH,
        )
        if pred is None:
            copy.wait_recv()
        else:
            pl.when(pred)(copy.wait_recv)

    def small(src, dst, s, r, dev):
        return pltpu.make_async_remote_copy(
            src_ref=src, dst_ref=dst, send_sem=tsend.at[s], recv_sem=trecv.at[r],
            device_id=dev, device_id_type=MESH,
        )

    own = []
    for r in range(rows):
        for h in range(2):
            src = v_ref.at[r, pl.ds(h * part, part)]
            send(None, src, z, x, r, h, {"panel": z_in})
            send(is_mid, src, z, x, r, h, {"panel": z_out})
            send(None, src, z, x, r, h, {"layer": xo})
    for r in range(rows):
        send_sib(None, v_ref.at[r], z, x, r)
        own.append(pltpu.make_async_copy(
            v_ref.at[r], xbuf.at[(z * 2 + c) * rows + r, pl.ds(x * half, half)], own_sem.at[r]))
        own[r].start()

    cols = cols_ref[...]
    lanes = lax.broadcasted_iota(jnp.int32, (rows, 128), 1)
    by_col = jnp.zeros((rows, 128), jnp.int32)
    by_slot = jnp.zeros((rows, 128), jnp.int32)
    for s in range(half):
        col = cols[:, s:s + 1]
        by_col = jnp.where(col == lanes, x * half + s + 1, by_col)
        by_slot = jnp.where(lanes == x * half + s, col, by_slot)
    rest = jnp.zeros((8 - 2 * rows, 128), jnp.int32)
    tq[x, c] = jnp.concatenate([by_col, by_slot, rest], axis=0)
    t1 = small(tq.at[x, c], tq.at[x, c], 0, 0, {"sub": co})
    t1.start()

    t1.wait_recv()
    t2 = small(tq.at[x], tq.at[x], 1, 1, {"layer": xo})
    t2.start()

    hi[zero_block] = jnp.zeros((blk, blk), jnp.bfloat16)
    lo[zero_block] = jnp.zeros((blk, blk), jnp.bfloat16)
    sq[...] = jnp.zeros_like(sq)

    t2.wait_recv()
    tz[z] = jnp.maximum(tq[0], tq[1])
    t3 = [
        small(tz.at[z], tz.at[z], 2 + d, 2 + z, {"panel": others[d]}) for d in range(3)
    ]
    for t in t3:
        t.start()

    def arrive(q, other, r, h, pred=None):
        zz = q_list[q]
        xx = xo if other else x
        wait_piece(zz, xx, r, h, pred)
        src = piece(zz, xx, c, r, h)

        def pass_on(p, dev):
            if p is None or pred is None or p is not pred:
                p = both(p, pred)
            send(p, src, zz, xx, r, h, dev)

        if other:
            if q == 0:
                pass_on(is_end, {"panel": z_in})
        elif q == 1:
            pass_on(is_mid, {"panel": z_in})
            if r == 0:
                pass_on(is_end, {"layer": xo})
        else:
            if pred is not is_end:
                pass_on(is_mid, {"panel": z_out})
            pass_on(None, {"layer": xo})
        if h == 1:
            send_sib(pred, row_piece(zz, xx, c, r), zz, xx, r)

    def group(*pieces, pred=None):
        for h in range(2):
            for q, other, r in pieces:
                arrive(q, other, r, h, pred)

    def late_extra():
        r = rows - 1
        for h in range(2):
            send(is_mid, piece(z, xo, c, r, h), z, xo, r, h, {"panel": z_out})

    def convert(row):
        val = xbuf[row]
        top = val.astype(jnp.bfloat16)
        hi[pl.ds(row * slots, slots)] = top
        lo[pl.ds(row * slots, slots)] = (val - top.astype(jnp.float32)).astype(jnp.bfloat16)

    def block_at(zz, cc, r, col):
        found = tabs[zz, cc, r, col]
        row = (zz * 2 + cc) * rows + r
        return jnp.where(found > 0, row * slots + found - 1, zero_block)

    def chunk_ready(q, r):
        zz = q_list[q]
        for xx in (x, xo):
            dst = row_piece(zz, xx, co, r)
            pltpu.make_async_remote_copy(
                src_ref=dst, dst_ref=dst, send_sem=send_sem.at[0],
                recv_sem=recv_sib.at[(zz * 2 + xx) * rows + r],
                device_id={"sub": co}, device_id_type=MESH,
            ).wait_recv()
        for cc in range(2):
            convert((zz * 2 + cc) * rows + r)

    def times(lh, ll, wh, wl):
        m = lh.shape[0]
        top = jnp.dot(jnp.concatenate([lh, ll], axis=0), wh, preferred_element_type=jnp.float32)
        return top[:m] + top[m:] + jnp.dot(lh, wl, preferred_element_type=jnp.float32)

    def chunk(*parts):
        from_rows = [(q_list[q], cc, r) for q, r in parts for cc in range(2)]

        def one_row(i, carry):
            lidx = [block_at(z, c, i, (zz * 2 + cc) * rows + r) for zz, cc, r in from_rows]
            lh = jnp.concatenate([hi[n] for n in lidx], axis=1)
            ll = jnp.concatenate([lo[n] for n in lidx], axis=1)
            for tp in range(slots // 2):
                cols = [tabs[z, c, 2 + i, 2 * tp + e] for e in range(2)]
                ridx = [[block_at(*row, col) for row in from_rows] for col in cols]
                wh = jnp.concatenate(
                    [jnp.concatenate([hi[n] for n in one], axis=0) for one in ridx], axis=1)
                wl = jnp.concatenate(
                    [jnp.concatenate([lo[n] for n in one], axis=0) for one in ridx], axis=1)
                sq[i, tp] += times(lh, ll, wh, wl)
            return carry

        lax.fori_loop(0, rows, one_row, 0)

    group((1, False, 0), (0, True, 0))
    group((2, False, 0), pred=is_mid)
    group((1, False, 1), (0, True, 1))
    group((2, False, 1), pred=is_mid)
    for zz in others:
        small(tz.at[zz], tz.at[zz], 2, 2 + zz, {"sub": co}).wait_recv()
    stage = pltpu.make_async_copy(tz, tabs, local_sem)
    stage.start()
    for r in range(rows):
        own[r].wait()
    chunk_ready(0, 0)
    chunk_ready(0, 1)
    stage.wait()
    group((2, False, 0), pred=is_end)
    chunk((0, 0), (0, 1))
    group((1, True, 0))
    group((3, False, 0), pred=is_mid)
    group((2, False, 1), pred=is_end)
    chunk_ready(1, 0)
    chunk((1, 0))
    group((2, True, 0))
    group((3, False, 1), pred=is_mid)
    late_extra()
    group((3, False, 0), pred=is_end)
    chunk_ready(2, 0)
    chunk((2, 0))
    group((2, True, 1))
    group((3, False, 1), pred=is_end)
    group((1, True, 1), pred=is_mid)
    chunk_ready(2, 1)
    chunk((2, 1))
    group((3, True, 0))
    chunk_ready(3, 0)
    chunk((3, 0))
    group((1, True, 1), pred=is_end)
    group((3, True, 1))
    chunk_ready(1, 1)
    chunk_ready(3, 1)
    chunk((3, 1), (1, 1))

    def cube_row(i):
        full = jnp.concatenate([sq[i, tp] for tp in range(slots // 2)], axis=1)
        sh = full.astype(jnp.bfloat16)
        sl = (full - sh.astype(jnp.float32)).astype(jnp.bfloat16)
        ks = [tabs[z, c, 2 + i, u] for u in range(slots)]
        for e in range(half // 2):
            cols = [tabs[z, c, 2 + i, x * half + 2 * e + f] for f in range(2)]
            idx = []
            for col in cols:
                one = []
                for k in ks:
                    found = tabs[k // (2 * rows), (k // rows) % 2, k % rows, col]
                    one.append(jnp.where(found > 0, k * slots + found - 1, zero_block))
                idx.append(one)
            wh = jnp.concatenate(
                [jnp.concatenate([hi[n] for n in one], axis=0) for one in idx], axis=1)
            wl = jnp.concatenate(
                [jnp.concatenate([lo[n] for n in one], axis=0) for one in idx], axis=1)
            res = 3.0 * sq[i, x * (half // 2) + e] - 2.0 * times(sh, sl, wh, wl)
            o_ref[i, 2 * e] = res[:, :blk]
            o_ref[i, 2 * e + 1] = res[:, blk:]

    for i in range(rows):
        cube_row(i)

    for t in (t1, t2, *t3):
        t.wait_send()
    for pred, copy in sends:
        if pred is None:
            copy.wait_send()
        else:
            pl.when(pred)(copy.wait_send)


def shards_kernel(values, columns):
    rows, half, blk, _ = values.shape
    slots, nb = 2 * half, 8 * rows
    return pl.pallas_call(
        kernel,
        out_shape=jax.ShapeDtypeStruct(values.shape, jnp.float32),
        in_specs=[
            pl.BlockSpec(memory_space=pltpu.VMEM),
            pl.BlockSpec(memory_space=pltpu.HBM),
        ],
        out_specs=pl.BlockSpec(memory_space=pltpu.VMEM),
        scratch_shapes=[
            pltpu.VMEM((nb, slots, blk, blk), jnp.float32),
            pltpu.VMEM((nb * slots + 1, blk, blk), jnp.bfloat16),
            pltpu.VMEM((nb * slots + 1, blk, blk), jnp.bfloat16),
            pltpu.VMEM((rows, slots // 2, blk, 2 * blk), jnp.float32),
            pltpu.VMEM((2, 2, 8, 128), jnp.int32),
            pltpu.VMEM((4, 2, 8, 128), jnp.int32),
            pltpu.SMEM((4, 2, 8, 128), jnp.int32),
            pltpu.SemaphoreType.DMA((96,)),
            pltpu.SemaphoreType.DMA((4 * 2 * rows * 2,)),
            pltpu.SemaphoreType.DMA((4 * 2 * rows * 2,)),
            pltpu.SemaphoreType.DMA((5,)),
            pltpu.SemaphoreType.DMA((6,)),
            pltpu.SemaphoreType.DMA,
            pltpu.SemaphoreType.DMA((rows,)),
        ],
        compiler_params=pltpu.CompilerParams(
            collective_id=0, has_side_effects=True, vmem_limit_bytes=48 * 1024 * 1024,
        ),
        cost_estimate=pl.CostEstimate(
            flops=3 * 2 * 3 * 64 * 2 * blk ** 3, bytes_accessed=2 * values.size * 4,
            transcendentals=0),
    )(columns, values)


def solution(mesh):
    shape = dict(mesh.shape)

    def shards(values, columns):
        fits = (shape["panel"], shape["layer"], shape["sub"]) == (4, 2, 2)
        if fits and values.shape == (2, 4, 128, 128):
            return shards_kernel(values, columns)
        return shards_general(values, columns)

    return jax.shard_map(
        shards,
        mesh=mesh,
        in_specs=(
            P(("groups", "panel", "sub"), "layer", None, None),
            P(("groups", "panel", "sub"), "layer"),
        ),
        out_specs=P(("groups", "panel", "sub"), "layer", None, None),
        check_vma=False,
    )
```
